32 devices in a mesh: groups: 2 (over x), chan: 16 (over z, y, core).
Axes of the slice: x: 2, y: 2, z: 4, core: 2. Of those that a mesh axis runs over, the one named last changes fastest.
Arguments:
- samples: bfloat16 [2048, 638], P(('groups', 'chan')), parts along dimension 0, may hold values from -6 to 6
- templates: bfloat16 [16, 64, 256], P('chan'), may hold values from -0.046875 to 0.046875
- moveouts: int32 [16, 64], P('chan'), may hold values from 0 to 255
- offsets: int32 [16], P('chan'), may hold values from 0 to 63, as said below
Outputs:
- stacks: float32 [32, 16, 128], P(('groups', 'chan')), parts along dimension 0
The draws below stay inside these ranges and needn't reach their ends.
There are 2 independent parts, one for each index of `groups`. The reference program is written for one: setup_inputs(seed, part) draws one part's arguments, and reference() takes and returns one part's arrays. A program takes and returns all parts, laid end to end along the dimension named above; an argument that names none is the same for every part. Nothing has to cross between parts.
Inputs may be any that keep to these rules, and one draw needn't show every extreme that they name: `offsets`: offset of a template's first channel from the start of a block of 64 channels; both 0 and 63 occur.
All inputs are finite; a program needn't handle non-finite values.
Results may differ from the reference program's by a relative error of at most 0.0003.
Values may be sent and summed in bfloat16 or wider, within the bound.
A program may use at most 64 MiB of HBM per device.

```python
import jax
import jax.numpy as jnp
from jax import lax

WIN = 64
TAPS = 256
MOVE = 256
TEMPLATES = 16
CHANNELS = 1024
SLAB = 638


def draw_offsets(key, part):
    key = jax.random.fold_in(key, 7)
    keys = jax.random.split(key, 3)
    values = jax.random.randint(keys[0], (TEMPLATES,), 0, WIN, dtype=jnp.int32)
    first = jax.random.randint(keys[1], (), 0, TEMPLATES, dtype=jnp.int32)
    second = (first + 1 + jax.random.randint(keys[2], (), 0, TEMPLATES - 1, dtype=jnp.int32)) % TEMPLATES
    return values.at[first].set(WIN - 1).at[second].set(0)


def touch_ends(entries, rng, smallest, top_value):
    index_at = [jax.random.randint(jax.random.fold_in(rng, axis), (), 0, length) for axis, length in enumerate(entries.shape)]
    main_axis = entries.shape.index(max(entries.shape))
    beside = index_at[:main_axis] + [(index_at[main_axis] + 1) % entries.shape[main_axis]] + index_at[main_axis + 1:]
    return entries.at[tuple(index_at)].set(smallest).at[tuple(beside)].set(top_value)


def block_levels(stream_key, shape, cuts, least, top_value):
    gain, own = 1.0, jax.random.fold_in(stream_key, 6)
    for axis_at, parts in cuts:
        steps = jnp.exp(jax.random.uniform(jax.random.fold_in(own, axis_at), (parts,), jnp.float32, least / len(cuts), top_value / len(cuts)))
        gain = gain * jnp.repeat(steps, shape[axis_at] // parts).reshape([-1 if axis == axis_at else 1 for axis in range(len(shape))])
    return gain


def centred(rng, shape, deviation, bound, cuts=(), kind=jnp.bfloat16):
    array = jax.random.normal(rng, shape, jnp.float32) * deviation
    if len(cuts) > 0:
        array = block_levels(rng, shape, cuts, -0.22, 0.18) * array
    return jnp.clip(array, min=-bound, max=bound).astype(kind)


def setup_inputs(seed: int = 0, part: int = 0) -> dict:
    streams_of = jax.random.split(jax.random.key(seed), 5)
    own_keys = jax.random.split(jax.random.fold_in(streams_of[4], part), 5)
    samples = centred(own_keys[0], (CHANNELS, SLAB), 1.0, 6.0, ((0, 16),))
    templates = centred(streams_of[1], (TEMPLATES, WIN, TAPS), (WIN * TAPS) ** -0.5, 0.046875, ((0, 16),))
    moveouts = touch_ends(jax.random.randint(streams_of[2], (TEMPLATES, WIN), 0, MOVE), jax.random.fold_in(streams_of[2], 1), 0, MOVE - 1).astype(jnp.int32)
    offsets = draw_offsets(jax.random.fold_in(streams_of[4], 71), part)
    return dict(samples=samples, templates=templates, moveouts=moveouts, offsets=offsets)


def reference(samples, templates, moveouts, offsets):
    channel_total = samples.shape[0]
    slab_length = samples.shape[1]
    lag_count = slab_length - TAPS - MOVE + 2
    padded = jnp.concatenate([samples.astype(jnp.float32), jnp.zeros((WIN, slab_length), jnp.float32)], 0)
    positions = jnp.arange(lag_count + TAPS - 1, dtype=jnp.int32)

    def single_template(entry):
        pattern, delays, offset = entry
        blocks = lax.dynamic_slice_in_dim(padded, offset.astype(jnp.int32), channel_total, 0)
        blocks = blocks.reshape(channel_total // WIN, WIN, slab_length)
        indices = positions[None, :] + delays.astype(jnp.int32)[:, None]
        indices = jnp.broadcast_to(indices[None], (blocks.shape[0],) + indices.shape)
        shifted = jnp.take_along_axis(blocks, indices, axis=2)
        result = lax.conv_general_dilated(shifted, pattern.astype(jnp.float32)[None], (1,), "VALID",
                                          dimension_numbers=("NCH", "OIH", "NCH"),
                                          precision=lax.Precision.HIGHEST,
                                          preferred_element_type=jnp.float32)
        return result[:, 0]

    stacks = lax.map(single_template, (templates, moveouts, offsets))
    return jnp.transpose(stacks, (1, 0, 2))
```

```python
import functools

import jax
import jax.numpy as jnp
from jax import lax
from jax.experimental import pallas as pl
from jax.experimental.pallas import tpu as pltpu
from jax.sharding import PartitionSpec as P

MOVE = 256
LANES = 128
ROWS = 16


def kernel(count, x_ref, h_ref, m_ref, off_ref, o_ref,
           buf, shifted, hankel, wide, r_out, r_in,
           a_send, a_recv, b_send, b_recv, r_send, r_recv):
    win, slab = x_ref.shape
    taps = h_ref.shape[2]
    chips = count // 2
    span = taps + MOVE
    padded = shifted.shape[0] * LANES
    packed_rows = buf.shape[1]
    me = lax.axis_index("chan")
    chip, core = me // 2, lax.rem(me, 2)
    sibling = 2 * chip + 1 - core
    before, after = lax.rem(me + count - 1, count), lax.rem(me + 1, count)
    across = lax.rem(me + 2 * core + count - 1, count)

    def far(step):
        return 2 * lax.rem(chip + step, chips) + core

    def near(step):
        return 2 * lax.rem(chip + chips - step, chips) + core

    barrier = pltpu.get_barrier_semaphore()
    pl.semaphore_signal(barrier, inc=1, device_id={"chan": sibling})
    pl.semaphore_signal(barrier, inc=1, device_id={"chan": across})

    @pl.loop(1, chips)
    def _(step):
        pl.semaphore_signal(barrier, inc=1, device_id={"chan": far(step)})

    offset = off_ref[0]
    row = lax.broadcasted_iota(jnp.int32, (win, win), 0)
    col = lax.broadcasted_iota(jnp.int32, (win, win), 1)
    turn = ((row - offset + win) % win == col).astype(jnp.float32).astype(jnp.bfloat16)
    buf[me, 0:win, :] = jnp.dot(turn, h_ref[0], preferred_element_type=jnp.float32).astype(jnp.bfloat16)
    row = lax.broadcasted_iota(jnp.int32, (win, LANES), 0)
    col = lax.broadcasted_iota(jnp.int32, (win, LANES), 1)
    turn = ((row == (col - offset + win) % win) & (col < win)).astype(jnp.float32).astype(jnp.bfloat16)
    moves = jnp.broadcast_to(m_ref[...].astype(jnp.float32), (ROWS, win)).astype(jnp.bfloat16)
    moves = jnp.dot(moves, turn, preferred_element_type=jnp.float32)
    lane = lax.broadcasted_iota(jnp.int32, (ROWS, LANES), 1)
    moves = jnp.where(lane == win, offset.astype(jnp.float32), moves)
    buf[me, win:packed_rows, 0:LANES] = moves.astype(jnp.bfloat16)
    buf[me, win:packed_rows, LANES:taps] = jnp.zeros((ROWS, taps - LANES), jnp.bfloat16)

    pl.semaphore_wait(barrier, chips + 1)

    def to_chip(step):
        return pltpu.make_async_remote_copy(
            src_ref=buf.at[me], dst_ref=buf.at[me], send_sem=a_send.at[step], recv_sem=a_recv.at[step],
            device_id={"chan": far(step)})

    def from_chip(step):
        return pltpu.make_async_remote_copy(
            src_ref=buf.at[near(step)], dst_ref=buf.at[near(step)], send_sem=a_send.at[step],
            recv_sem=a_recv.at[step], device_id={"chan": far(step)})

    def to_sibling(step):
        return pltpu.make_async_remote_copy(
            src_ref=buf.at[near(step)], dst_ref=buf.at[near(step)], send_sem=b_send.at[step],
            recv_sem=b_recv.at[step], device_id={"chan": sibling})

    def from_sibling(step):
        slot = near(step) + 1 - 2 * core
        return pltpu.make_async_remote_copy(
            src_ref=buf.at[slot], dst_ref=buf.at[slot], send_sem=b_send.at[step],
            recv_sem=b_recv.at[step], device_id={"chan": sibling})

    @pl.loop(1, chips)
    def _(step):
        to_chip(step).start()

    to_sibling(0).start()

    samples = jnp.concatenate(
        [x_ref[...].astype(jnp.float32), jnp.zeros((win, padded - slab), jnp.float32)], 1)
    for r in range(ROWS):
        moved = samples if r == 0 else pltpu.roll(samples, padded - r, 1)
        for a in range(padded // LANES):
            shifted[a, r * win:(r + 1) * win, :] = moved[:, a * LANES:(a + 1) * LANES]

    @pl.loop(0, win)
    def _(c):
        slopes = jnp.concatenate(
            [shifted[a, pl.ds(c, ROWS, stride=win), :] for a in range(padded // LANES)], 1).astype(jnp.bfloat16)
        for b in range(LANES // ROWS):
            moved = slopes[:, b * ROWS:b * ROWS + span]
            for a in range(span // LANES):
                at = pl.multiple_of(c * span + a * LANES + b * ROWS, ROWS)
                hankel[pl.ds(at, ROWS), :] = moved[:, a * LANES:(a + 1) * LANES]

    @pl.loop(1, chips)
    def _(step):
        from_chip(step).wait_recv()
        to_sibling(step).start()

    def widen(slot):
        rows = pl.ds(pl.multiple_of(slot * packed_rows, 8), packed_rows)
        for a in range(taps // LANES):
            wide[a, rows, :] = buf[slot, :, a * LANES:(a + 1) * LANES].astype(jnp.float32)

    @pl.loop(0, chips)
    def _(step):
        widen(near(step))

    @pl.loop(0, chips)
    def _(step):
        from_sibling(step).wait_recv()
        widen(near(step) + 1 - 2 * core)

    meta = wide[0, pl.ds(win, count, stride=packed_rows), :]
    lane = lax.broadcasted_iota(jnp.int32, (count, LANES), 1)
    offsets = jnp.sum(jnp.where(lane == win, meta, 0.0), 1, keepdims=True).astype(jnp.int32)

    def channel(c, total):
        low = wide[0, pl.ds(c, count, stride=packed_rows), :]
        high = wide[1, pl.ds(c, count, stride=packed_rows), :]
        move = jnp.sum(jnp.where(lane == c, meta, 0.0), 1, keepdims=True).astype(jnp.int32)
        move = jnp.broadcast_to(move, (count, LANES))
        part = move & (LANES - 1)
        index = (lane - part) & (LANES - 1)
        low = jnp.take_along_axis(low, index, 1)
        high = jnp.take_along_axis(high, index, 1)
        inside, late = lane >= part, move >= LANES
        own = jnp.broadcast_to(offsets, (count, LANES)) <= c
        first = jnp.where(inside, low, 0.0)
        second = jnp.where(inside, high, low)
        third = jnp.where(inside, 0.0, high)
        tiles = [jnp.where(late, 0.0, first), jnp.where(late, first, second),
                 jnp.where(late, second, third), jnp.where(late, third, 0.0)]
        here = jnp.concatenate([jnp.where(own, t, 0.0) for t in tiles], 1).astype(jnp.bfloat16)
        there = jnp.concatenate([jnp.where(own, 0.0, t) for t in tiles], 1).astype(jnp.bfloat16)
        both = jnp.concatenate([here, there], 0)
        block = hankel[pl.ds(pl.multiple_of(c * span, span), span), :]
        return total + jnp.dot(both, block, preferred_element_type=jnp.float32)

    total = lax.fori_loop(0, win, channel, jnp.zeros((2 * count, LANES), jnp.float32), unroll=2)

    r_out[...] = total[count:]
    send = pltpu.make_async_remote_copy(
        src_ref=r_out, dst_ref=r_in, send_sem=r_send, recv_sem=r_recv, device_id={"chan": before})
    send.start()

    @pl.loop(1, chips)
    def _(step):
        to_chip(step).wait_send()

    @pl.loop(0, chips)
    def _(step):
        to_sibling(step).wait_send()

    send.wait_recv()
    last = me == count - 1
    o_ref[0] = total[:count] + jnp.where(last, 0.0, r_in[...])
    send.wait_send()


def per_device(samples, templates, moveouts, offsets):
    win, slab = samples.shape
    taps = templates.shape[2]
    count = lax.axis_size("chan")
    lags = slab - taps - MOVE + 2
    chips = count // 2
    span = taps + MOVE
    padded = -(-(slab + 1) // LANES) * LANES
    packed_rows = win + ROWS
    vmem = pl.BlockSpec(memory_space=pltpu.VMEM)
    return pl.pallas_call(
        functools.partial(kernel, count),
        out_shape=jax.ShapeDtypeStruct((1, count, lags), jnp.float32),
        in_specs=[vmem, vmem, vmem, pl.BlockSpec(memory_space=pltpu.SMEM)],
        out_specs=vmem,
        scratch_shapes=[
            pltpu.VMEM((count, packed_rows, taps), jnp.bfloat16),
            pltpu.VMEM((padded // LANES, ROWS * win, LANES), jnp.float32),
            pltpu.VMEM((win * span, LANES), jnp.bfloat16),
            pltpu.VMEM((taps // LANES, count * packed_rows, LANES), jnp.float32),
            pltpu.VMEM((count, LANES), jnp.float32),
            pltpu.VMEM((count, LANES), jnp.float32),
            pltpu.SemaphoreType.DMA((chips,)),
            pltpu.SemaphoreType.DMA((chips,)),
            pltpu.SemaphoreType.DMA((chips,)),
            pltpu.SemaphoreType.DMA((chips,)),
            pltpu.SemaphoreType.DMA,
            pltpu.SemaphoreType.DMA,
        ],
        compiler_params=pltpu.CompilerParams(
            collective_id=0, has_side_effects=True, vmem_limit_bytes=48 * 2**20),
        cost_estimate=pl.CostEstimate(
            flops=4 * count * win * span * lags, bytes_accessed=4 * win * slab, transcendentals=0),
    )(samples, templates, moveouts, offsets)


def solution(mesh):
    in_specs = (P(("groups", "chan"), None), P("chan", None, None), P("chan", None), P("chan"))
    out_specs = P(("groups", "chan"), None, None)
    return jax.shard_map(
        per_device, mesh=mesh, in_specs=in_specs, out_specs=out_specs, check_vma=False
    )
```

```python
import functools

import jax
import jax.numpy as jnp
from jax import lax
from jax.experimental import pallas as pl
from jax.experimental.pallas import tpu as pltpu
from jax.sharding import PartitionSpec as P

MOVE = 256
LANES = 128
ROWS = 16


def kernel(count, x_ref, h_ref, m_ref, off_ref, o_ref,
           buf, shifted, hankel, wide, r_out, r_in,
           a_send, a_recv, b_send, b_recv, r_send, r_recv):
    win, slab = x_ref.shape
    taps = h_ref.shape[2]
    chips = count // 2
    span = taps + MOVE
    padded = shifted.shape[0] * LANES
    packed_rows = buf.shape[1]
    me = lax.axis_index("chan")
    chip, core = me // 2, lax.rem(me, 2)
    sibling = 2 * chip + 1 - core
    before, after = lax.rem(me + count - 1, count), lax.rem(me + 1, count)
    across = lax.rem(me + 2 * core + count - 1, count)

    def far(step):
        return 2 * lax.rem(chip + step, chips) + core

    def near(step):
        return 2 * lax.rem(chip + chips - step, chips) + core

    barrier = pltpu.get_barrier_semaphore()
    pl.semaphore_signal(barrier, inc=1, device_id={"chan": sibling})
    pl.semaphore_signal(barrier, inc=1, device_id={"chan": across})

    @pl.loop(1, chips)
    def _(step):
        pl.semaphore_signal(barrier, inc=1, device_id={"chan": far(step)})

    offset = off_ref[0]
    row = lax.broadcasted_iota(jnp.int32, (win, win), 0)
    col = lax.broadcasted_iota(jnp.int32, (win, win), 1)
    turn = ((row - offset + win) % win == col).astype(jnp.float32).astype(jnp.bfloat16)
    buf[me, 0:win, :] = jnp.dot(turn, h_ref[0], preferred_element_type=jnp.float32).astype(jnp.bfloat16)
    row = lax.broadcasted_iota(jnp.int32, (win, LANES), 0)
    col = lax.broadcasted_iota(jnp.int32, (win, LANES), 1)
    turn = ((row == (col - offset + win) % win) & (col < win)).astype(jnp.float32).astype(jnp.bfloat16)
    moves = jnp.broadcast_to(m_ref[...].astype(jnp.float32), (ROWS, win)).astype(jnp.bfloat16)
    moves = jnp.dot(moves, turn, preferred_element_type=jnp.float32)
    lane = lax.broadcasted_iota(jnp.int32, (ROWS, LANES), 1)
    moves = jnp.where(lane == win, offset.astype(jnp.float32), moves)
    buf[me, win:packed_rows, 0:LANES] = moves.astype(jnp.bfloat16)
    buf[me, win:packed_rows, LANES:taps] = jnp.zeros((ROWS, taps - LANES), jnp.bfloat16)

    pl.semaphore_wait(barrier, chips + 1)

    def to_chip(step):
        return pltpu.make_async_remote_copy(
            src_ref=buf.at[me], dst_ref=buf.at[me], send_sem=a_send.at[step], recv_sem=a_recv.at[step],
            device_id={"chan": far(step)})

    def from_chip(step):
        return pltpu.make_async_remote_copy(
            src_ref=buf.at[near(step)], dst_ref=buf.at[near(step)], send_sem=a_send.at[step],
            recv_sem=a_recv.at[step], device_id={"chan": far(step)})

    def to_sibling(step):
        return pltpu.make_async_remote_copy(
            src_ref=buf.at[near(step)], dst_ref=buf.at[near(step)], send_sem=b_send.at[step],
            recv_sem=b_recv.at[step], device_id={"chan": sibling})

    def from_sibling(step):
        slot = near(step) + 1 - 2 * core
        return pltpu.make_async_remote_copy(
            src_ref=buf.at[slot], dst_ref=buf.at[slot], send_sem=b_send.at[step],
            recv_sem=b_recv.at[step], device_id={"chan": sibling})

    @pl.loop(1, chips)
    def _(step):
        to_chip(step).start()

    to_sibling(0).start()

    samples = jnp.concatenate(
        [x_ref[...].astype(jnp.float32), jnp.zeros((win, padded - slab), jnp.float32)], 1)
    for r in range(ROWS):
        moved = samples if r == 0 else pltpu.roll(samples, padded - r, 1)
        for a in range(padded // LANES):
            shifted[a, r * win:(r + 1) * win, :] = moved[:, a * LANES:(a + 1) * LANES]

    @pl.loop(0, win, unroll=8)
    def _(c):
        slopes = jnp.concatenate(
            [shifted[a, pl.ds(c, ROWS, stride=win), :] for a in range(padded // LANES)], 1).astype(jnp.bfloat16)
        for b in range(LANES // ROWS):
            moved = slopes[:, b * ROWS:b * ROWS + span]
            for a in range(span // LANES):
                at = pl.multiple_of(c * span + a * LANES + b * ROWS, ROWS)
                hankel[pl.ds(at, ROWS), :] = moved[:, a * LANES:(a + 1) * LANES]

    @pl.loop(1, chips)
    def _(step):
        from_chip(step).wait_recv()
        to_sibling(step).start()

    def widen(slot):
        rows = pl.ds(pl.multiple_of(slot * packed_rows, 8), packed_rows)
        for a in range(taps // LANES):
            wide[a, rows, :] = buf[slot, :, a * LANES:(a + 1) * LANES].astype(jnp.float32)

    @pl.loop(0, chips)
    def _(step):
        widen(near(step))

    @pl.loop(0, chips)
    def _(step):
        from_sibling(step).wait_recv()
        widen(near(step) + 1 - 2 * core)

    meta = wide[0, pl.ds(win, count, stride=packed_rows), :]
    lane = lax.broadcasted_iota(jnp.int32, (count, LANES), 1)
    offsets = jnp.sum(jnp.where(lane == win, meta, 0.0), 1, keepdims=True).astype(jnp.int32)

    def channel(c, total):
        low = wide[0, pl.ds(c, count, stride=packed_rows), :]
        high = wide[1, pl.ds(c, count, stride=packed_rows), :]
        move = jnp.sum(jnp.where(lane == c, meta, 0.0), 1, keepdims=True).astype(jnp.int32)
        move = jnp.broadcast_to(move, (count, LANES))
        part = move & (LANES - 1)
        index = (lane - part) & (LANES - 1)
        low = jnp.take_along_axis(low, index, 1)
        high = jnp.take_along_axis(high, index, 1)
        inside, late = lane >= part, move >= LANES
        own = jnp.broadcast_to(offsets, (count, LANES)) <= c
        first = jnp.where(inside, low, 0.0)
        second = jnp.where(inside, high, low)
        third = jnp.where(inside, 0.0, high)
        tiles = [jnp.where(late, 0.0, first), jnp.where(late, first, second),
                 jnp.where(late, second, third), jnp.where(late, third, 0.0)]
        here = jnp.concatenate([jnp.where(own, t, 0.0) for t in tiles], 1).astype(jnp.bfloat16)
        there = jnp.concatenate([jnp.where(own, 0.0, t) for t in tiles], 1).astype(jnp.bfloat16)
        both = jnp.concatenate([here, there], 0)
        block = hankel[pl.ds(pl.multiple_of(c * span, span), span), :]
        return total + jnp.dot(both, block, preferred_element_type=jnp.float32)

    total = lax.fori_loop(0, win, channel, jnp.zeros((2 * count, LANES), jnp.float32), unroll=8)

    r_out[...] = total[count:]
    send = pltpu.make_async_remote_copy(
        src_ref=r_out, dst_ref=r_in, send_sem=r_send, recv_sem=r_recv, device_id={"chan": before})
    send.start()

    @pl.loop(1, chips)
    def _(step):
        to_chip(step).wait_send()

    @pl.loop(0, chips)
    def _(step):
        to_sibling(step).wait_send()

    send.wait_recv()
    last = me == count - 1
    o_ref[0] = total[:count] + jnp.where(last, 0.0, r_in[...])
    send.wait_send()


def per_device(samples, templates, moveouts, offsets):
    win, slab = samples.shape
    taps = templates.shape[2]
    count = lax.axis_size("chan")
    lags = slab - taps - MOVE + 2
    chips = count // 2
    span = taps + MOVE
    padded = -(-(slab + 1) // LANES) * LANES
    packed_rows = win + ROWS
    vmem = pl.BlockSpec(memory_space=pltpu.VMEM)
    return pl.pallas_call(
        functools.partial(kernel, count),
        out_shape=jax.ShapeDtypeStruct((1, count, lags), jnp.float32),
        in_specs=[vmem, vmem, vmem, pl.BlockSpec(memory_space=pltpu.SMEM)],
        out_specs=vmem,
        scratch_shapes=[
            pltpu.VMEM((count, packed_rows, taps), jnp.bfloat16),
            pltpu.VMEM((padded // LANES, ROWS * win, LANES), jnp.float32),
            pltpu.VMEM((win * span, LANES), jnp.bfloat16),
            pltpu.VMEM((taps // LANES, count * packed_rows, LANES), jnp.float32),
            pltpu.VMEM((count, LANES), jnp.float32),
            pltpu.VMEM((count, LANES), jnp.float32),
            pltpu.SemaphoreType.DMA((chips,)),
            pltpu.SemaphoreType.DMA((chips,)),
            pltpu.SemaphoreType.DMA((chips,)),
            pltpu.SemaphoreType.DMA((chips,)),
            pltpu.SemaphoreType.DMA,
            pltpu.SemaphoreType.DMA,
        ],
        compiler_params=pltpu.CompilerParams(
            collective_id=0, has_side_effects=True, vmem_limit_bytes=48 * 2**20),
        cost_estimate=pl.CostEstimate(
            flops=4 * count * win * span * lags, bytes_accessed=4 * win * slab, transcendentals=0),
    )(samples, templates, moveouts, offsets)


def solution(mesh):
    in_specs = (P(("groups", "chan"), None), P("chan", None, None), P("chan", None), P("chan"))
    out_specs = P(("groups", "chan"), None, None)
    return jax.shard_map(
        per_device, mesh=mesh, in_specs=in_specs, out_specs=out_specs, check_vma=False
    )
```

```python
import functools

import jax
import jax.numpy as jnp
from jax import lax
from jax.experimental import pallas as pl
from jax.experimental.pallas import tpu as pltpu
from jax.sharding import PartitionSpec as P

MOVE = 256
LANES = 128
ROWS = 16


def kernel(count, x_ref, h_ref, m_ref, off_ref, o_ref,
           buf, shifted, hankel, wide, r_out, r_in,
           a_send, a_recv, b_send, b_recv, r_send, r_recv):
    win, slab = x_ref.shape
    taps = h_ref.shape[2]
    chips = count // 2
    span = taps + MOVE
    padded = shifted.shape[0] * LANES
    packed_rows = buf.shape[1]
    me = lax.axis_index("chan")
    chip, core = me // 2, lax.rem(me, 2)
    sibling = 2 * chip + 1 - core
    before, after = lax.rem(me + count - 1, count), lax.rem(me + 1, count)
    across = lax.rem(me + 2 * core + count - 1, count)

    def far(step):
        return 2 * lax.rem(chip + step, chips) + core

    def near(step):
        return 2 * lax.rem(chip + chips - step, chips) + core

    barrier = pltpu.get_barrier_semaphore()
    pl.semaphore_signal(barrier, inc=1, device_id={"chan": sibling})
    pl.semaphore_signal(barrier, inc=1, device_id={"chan": across})

    @pl.loop(1, chips)
    def _(step):
        pl.semaphore_signal(barrier, inc=1, device_id={"chan": far(step)})

    offset = off_ref[0]
    row = lax.broadcasted_iota(jnp.int32, (win, win), 0)
    col = lax.broadcasted_iota(jnp.int32, (win, win), 1)
    turn = ((row - offset + win) % win == col).astype(jnp.float32).astype(jnp.bfloat16)
    buf[me, 0:win, :] = jnp.dot(turn, h_ref[0], preferred_element_type=jnp.float32).astype(jnp.bfloat16)
    row = lax.broadcasted_iota(jnp.int32, (win, LANES), 0)
    col = lax.broadcasted_iota(jnp.int32, (win, LANES), 1)
    turn = ((row == (col - offset + win) % win) & (col < win)).astype(jnp.float32).astype(jnp.bfloat16)
    moves = jnp.broadcast_to(m_ref[...].astype(jnp.float32), (ROWS, win)).astype(jnp.bfloat16)
    moves = jnp.dot(moves, turn, preferred_element_type=jnp.float32)
    lane = lax.broadcasted_iota(jnp.int32, (ROWS, LANES), 1)
    moves = jnp.where(lane == win, offset.astype(jnp.float32), moves)
    buf[me, win:packed_rows, 0:LANES] = moves.astype(jnp.bfloat16)
    buf[me, win:packed_rows, LANES:taps] = jnp.zeros((ROWS, taps - LANES), jnp.bfloat16)

    pl.semaphore_wait(barrier, chips + 1)

    def to_chip(step):
        return pltpu.make_async_remote_copy(
            src_ref=buf.at[me], dst_ref=buf.at[me], send_sem=a_send.at[step], recv_sem=a_recv.at[step],
            device_id={"chan": far(step)})

    def from_chip(step):
        return pltpu.make_async_remote_copy(
            src_ref=buf.at[near(step)], dst_ref=buf.at[near(step)], send_sem=a_send.at[step],
            recv_sem=a_recv.at[step], device_id={"chan": far(step)})

    def to_sibling(step):
        return pltpu.make_async_remote_copy(
            src_ref=buf.at[near(step)], dst_ref=buf.at[near(step)], send_sem=b_send.at[step],
            recv_sem=b_recv.at[step], device_id={"chan": sibling})

    def from_sibling(step):
        slot = near(step) + 1 - 2 * core
        return pltpu.make_async_remote_copy(
            src_ref=buf.at[slot], dst_ref=buf.at[slot], send_sem=b_send.at[step],
            recv_sem=b_recv.at[step], device_id={"chan": sibling})

    @pl.loop(1, chips)
    def _(step):
        to_chip(step).start()

    to_sibling(0).start()

    samples = jnp.concatenate(
        [x_ref[...].astype(jnp.float32), jnp.zeros((win, padded - slab), jnp.float32)], 1)
    for r in range(ROWS):
        moved = samples if r == 0 else pltpu.roll(samples, padded - r, 1)
        for a in range(padded // LANES):
            shifted[a, r * win:(r + 1) * win, :] = moved[:, a * LANES:(a + 1) * LANES]

    @pl.loop(0, win, unroll=16)
    def _(c):
        slopes = jnp.concatenate(
            [shifted[a, pl.ds(c, ROWS, stride=win), :] for a in range(padded // LANES)], 1).astype(jnp.bfloat16)
        for b in range(LANES // ROWS):
            moved = slopes[:, b * ROWS:b * ROWS + span]
            for a in range(span // LANES):
                at = pl.multiple_of(c * span + a * LANES + b * ROWS, ROWS)
                hankel[pl.ds(at, ROWS), :] = moved[:, a * LANES:(a + 1) * LANES]

    @pl.loop(1, chips)
    def _(step):
        from_chip(step).wait_recv()
        to_sibling(step).start()

    def widen(slot):
        rows = pl.ds(pl.multiple_of(slot * packed_rows, 8), packed_rows)
        for a in range(taps // LANES):
            wide[a, rows, :] = buf[slot, :, a * LANES:(a + 1) * LANES].astype(jnp.float32)

    @pl.loop(0, chips)
    def _(step):
        widen(near(step))

    @pl.loop(0, chips)
    def _(step):
        from_sibling(step).wait_recv()
        widen(near(step) + 1 - 2 * core)

    meta = wide[0, pl.ds(win, count, stride=packed_rows), :]
    lane = lax.broadcasted_iota(jnp.int32, (count, LANES), 1)
    offsets = jnp.sum(jnp.where(lane == win, meta, 0.0), 1, keepdims=True).astype(jnp.int32)

    def channel(c, total):
        low = wide[0, pl.ds(c, count, stride=packed_rows), :]
        high = wide[1, pl.ds(c, count, stride=packed_rows), :]
        move = jnp.sum(jnp.where(lane == c, meta, 0.0), 1, keepdims=True).astype(jnp.int32)
        move = jnp.broadcast_to(move, (count, LANES))
        part = move & (LANES - 1)
        index = (lane - part) & (LANES - 1)
        low = jnp.take_along_axis(low, index, 1)
        high = jnp.take_along_axis(high, index, 1)
        inside, late = lane >= part, move >= LANES
        own = jnp.broadcast_to(offsets, (count, LANES)) <= c
        first = jnp.where(inside, low, 0.0)
        second = jnp.where(inside, high, low)
        third = jnp.where(inside, 0.0, high)
        tiles = [jnp.where(late, 0.0, first), jnp.where(late, first, second),
                 jnp.where(late, second, third), jnp.where(late, third, 0.0)]
        here = jnp.concatenate([jnp.where(own, t, 0.0) for t in tiles], 1).astype(jnp.bfloat16)
        there = jnp.concatenate([jnp.where(own, 0.0, t) for t in tiles], 1).astype(jnp.bfloat16)
        both = jnp.concatenate([here, there], 0)
        block = hankel[pl.ds(pl.multiple_of(c * span, span), span), :]
        return total + jnp.dot(both, block, preferred_element_type=jnp.float32)

    total = lax.fori_loop(0, win, channel, jnp.zeros((2 * count, LANES), jnp.float32), unroll=16)

    r_out[...] = total[count:]
    send = pltpu.make_async_remote_copy(
        src_ref=r_out, dst_ref=r_in, send_sem=r_send, recv_sem=r_recv, device_id={"chan": before})
    send.start()

    @pl.loop(1, chips)
    def _(step):
        to_chip(step).wait_send()

    @pl.loop(0, chips)
    def _(step):
        to_sibling(step).wait_send()

    send.wait_recv()
    last = me == count - 1
    o_ref[0] = total[:count] + jnp.where(last, 0.0, r_in[...])
    send.wait_send()


def per_device(samples, templates, moveouts, offsets):
    win, slab = samples.shape
    taps = templates.shape[2]
    count = lax.axis_size("chan")
    lags = slab - taps - MOVE + 2
    chips = count // 2
    span = taps + MOVE
    padded = -(-(slab + 1) // LANES) * LANES
    packed_rows = win + ROWS
    vmem = pl.BlockSpec(memory_space=pltpu.VMEM)
    return pl.pallas_call(
        functools.partial(kernel, count),
        out_shape=jax.ShapeDtypeStruct((1, count, lags), jnp.float32),
        in_specs=[vmem, vmem, vmem, pl.BlockSpec(memory_space=pltpu.SMEM)],
        out_specs=vmem,
        scratch_shapes=[
            pltpu.VMEM((count, packed_rows, taps), jnp.bfloat16),
            pltpu.VMEM((padded // LANES, ROWS * win, LANES), jnp.float32),
            pltpu.VMEM((win * span, LANES), jnp.bfloat16),
            pltpu.VMEM((taps // LANES, count * packed_rows, LANES), jnp.float32),
            pltpu.VMEM((count, LANES), jnp.float32),
            pltpu.VMEM((count, LANES), jnp.float32),
            pltpu.SemaphoreType.DMA((chips,)),
            pltpu.SemaphoreType.DMA((chips,)),
            pltpu.SemaphoreType.DMA((chips,)),
            pltpu.SemaphoreType.DMA((chips,)),
            pltpu.SemaphoreType.DMA,
            pltpu.SemaphoreType.DMA,
        ],
        compiler_params=pltpu.CompilerParams(
            collective_id=0, has_side_effects=True, vmem_limit_bytes=48 * 2**20),
        cost_estimate=pl.CostEstimate(
            flops=4 * count * win * span * lags, bytes_accessed=4 * win * slab, transcendentals=0),
    )(samples, templates, moveouts, offsets)


def solution(mesh):
    in_specs = (P(("groups", "chan"), None), P("chan", None, None), P("chan", None), P("chan"))
    out_specs = P(("groups", "chan"), None, None)
    return jax.shard_map(
        per_device, mesh=mesh, in_specs=in_specs, out_specs=out_specs, check_vma=False
    )
```
